256 devices in a mesh: ell: 32 (over x, y, core), rad: 8 (over z).
Axes of the slice: x: 4, y: 4, z: 8, core: 2. Of those that a mesh axis runs over, the one named last changes fastest.
Arguments:
- shells: bfloat16 [1024, 1024, 128], P('ell', 'rad'), may hold values from -6 to 6
- start_values: float32 [1024, 1024], P('ell', 'rad'), may hold values from 0.01 to 0.09
- rec_scale: float32 [1024, 512], P('ell'), may hold values from 1.7 to 1.9
- rec_shift: float32 [1024, 512], P('ell'), may hold values from -0.05 to 0.05
- rec_damp: float32 [1024, 512], P('ell'), may hold values from 0.996 to 1
- degree_counts: int32 [1024], P('ell'), may hold values from 1 to 512
- owners: int32 [1024], P('ell'), may hold values from 0 to 31, as said below
Outputs:
- coefficients: float32 [1024, 512, 128], P('ell', 'rad')
The draws below stay inside these ranges and needn't reach their ends.
Inputs may be any that keep to these rules, and one draw needn't show every extreme that they name: `owners`: in every run of 32 ells that starts at a multiple of 32, every owner index appears exactly 1 times.
All inputs are finite; a program needn't handle non-finite values.
Results may differ from the reference program's by a relative error of at most 0.0018.
The reference program's roundings to bfloat16 on the way (of `tables`) count: a program that leaves them out, or rounds other values in their place, can miss the bound.
Values may be sent and summed in bfloat16 or wider, within the bound.
A program may use at most 64 MiB of HBM per device.

```python
import math
import jax
import jax.numpy as jnp
from jax import lax

L = 1024
R = 1024
NDEG = 512
C = 128
OWNED = 32
SHARE = 1


def draw_owners(key, part):
    keys = jax.random.split(jax.random.fold_in(key, 11), L // OWNED)
    shuffled = jax.vmap(lambda single: jax.random.permutation(single, OWNED))(keys)
    return (shuffled // SHARE).reshape(L).astype(jnp.int32)


def draw_degree_counts(key, part):
    degree = jnp.arange(L, dtype=jnp.int32)
    jitter = jax.random.randint(jax.random.fold_in(key, 23), (L,), 0, 4, dtype=jnp.int32)
    jitter = jnp.where(degree == 0, 0, jitter)
    return jnp.maximum(NDEG - degree * NDEG // L - jitter, 1).astype(jnp.int32)


def steps_of(rng, dims, shards, smallest, largest):
    loudness, own = 1.0, jax.random.fold_in(rng, 6)
    for dim, parts in shards:
        heights = jnp.exp(jax.random.uniform(jax.random.fold_in(own, dim), (parts,), jnp.float32, smallest / len(shards), largest / len(shards)))
        loudness = loudness * jnp.repeat(heights, dims[dim] // parts).reshape([-1 if axis == dim else 1 for axis in range(len(dims))])
    return loudness


def gaussian(stream_key, dims, width, limit, shards=(), kind=jnp.bfloat16):
    result = jax.random.normal(stream_key, dims, jnp.float32) * width
    if len(shards) > 0:
        result = steps_of(stream_key, dims, shards, -0.22, 0.18) * result
    return jnp.clip(result, min=-limit, max=limit).astype(kind)


def setup_inputs(seed: int = 0) -> dict:
    key_list = jax.random.split(jax.random.key(seed), 8)
    return {
        "shells": gaussian(key_list[0], (L, R, C), 1.0, 6.0, ((0, 32), (1, 8))),
        "start_values": jnp.clip(jnp.exp(math.log(0.09) - 2.1972246 * jax.random.uniform(key_list[1], (L, R), jnp.float32) ** steps_of(key_list[1], (L, R), ((0, 32), (1, 8)), -0.2, 0.2)), 0.01, 0.09),
        "rec_scale": jnp.clip(1.7 + 0.19999993 * jax.random.uniform(key_list[2], (L, NDEG), jnp.float32) ** steps_of(key_list[2], (L, NDEG), ((0, 32),), -0.2, 0.2), 1.7, 1.9),
        "rec_shift": jnp.clip(jax.random.uniform(key_list[3], (L, NDEG), jnp.float32, -0.05, 0.05) * steps_of(key_list[3], (L, NDEG), ((0, 32),), -0.4, 0.0), -0.05, 0.05),
        "rec_damp": jnp.clip(0.996 + 0.004000008 * jax.random.uniform(key_list[4], (L, NDEG), jnp.float32) ** steps_of(key_list[4], (L, NDEG), ((0, 32),), -0.2, 0.2), 0.996, 1.0),
        "degree_counts": draw_degree_counts(jax.random.fold_in(key_list[7], 71), 0),
        "owners": draw_owners(jax.random.fold_in(key_list[7], 71), 0),
    }


def radial_nodes(count_r):
    index = jnp.arange(count_r, dtype=jnp.int32).astype(jnp.float32)
    return jnp.cos(jnp.pi * (2.0 * index + 1.0) / (2.0 * R))


def build_tables(start_values, rec_scale, rec_shift, rec_damp, degree_counts, nodes):
    ndeg = rec_scale.shape[1]
    first = start_values
    second = rec_scale[:, 0:1] * (nodes[None, :] + rec_shift[:, 0:1]) * first

    def advance(carry, inputs):
        previous, current = carry
        scale, shift, damp = inputs
        upcoming = scale[:, None] * (nodes[None, :] + shift[:, None]) * current - damp[:, None] * previous
        return (current, upcoming), upcoming

    rest = lax.scan(advance, (first, second), (rec_scale[:, 1:ndeg - 1].T, rec_shift[:, 1:ndeg - 1].T, rec_damp[:, 1:ndeg - 1].T))[1]
    tables = jnp.concatenate([first[None], second[None], rest], axis=0)
    degree = jnp.arange(ndeg, dtype=jnp.int32)
    live = degree[:, None] < degree_counts[None, :]
    tables = jnp.where(live[:, :, None], tables, jnp.zeros_like(tables))
    return tables.astype(jnp.bfloat16)


def reference(shells, start_values, rec_scale, rec_shift, rec_damp, degree_counts, owners):
    block = min(64, L)
    nodes = radial_nodes(R)

    def one_block(inputs):
        data, start, scale, shift, damp, counts = inputs
        tables = build_tables(start, scale, shift, damp, counts, nodes)
        return jnp.einsum("nei,eic->enc", tables.astype(jnp.float32), data.astype(jnp.float32))

    blocks = L // block
    transformed = lax.map(one_block, (shells.reshape(blocks, block, R, C), start_values.reshape(blocks, block, R), rec_scale.reshape(blocks, block, NDEG), rec_shift.reshape(blocks, block, NDEG), rec_damp.reshape(blocks, block, NDEG), degree_counts.reshape(blocks, block)))
    transformed = transformed.reshape(L, NDEG, C)
    grouped = owners.reshape(L // OWNED, OWNED)
    same = grouped[:, :, None] == grouped[:, None, :]
    position = jnp.arange(OWNED, dtype=jnp.int32)
    before = position[None, :] < position[:, None]
    rank = jnp.sum(jnp.logical_and(same, before[None]).astype(jnp.int32), axis=2).astype(jnp.int32)
    slabs = jnp.arange(L // OWNED, dtype=jnp.int32)
    slot = grouped * OWNED + slabs[:, None] * SHARE + rank
    order = jnp.argsort(slot.reshape(L))
    return transformed[order]
```

```python
import jax
import jax.numpy as jnp
from jax import lax
from jax.experimental import pallas as pl
from jax.experimental.pallas import tpu as pltpu
from jax.sharding import PartitionSpec as P

MESH = pl.DeviceIdType.MESH
R = 1024
NDEG = 512
C = 128
NX, NY, NC, NZ = 4, 4, 2, 8
GROUPS = NX * NY * NC
PER = GROUPS // NZ
BLOCK = R // NZ
SHARE = NDEG // NZ


def ell_index(x, y, core):
    return (lax.rem(x + 2 * NX, NX) * NY + lax.rem(y + 2 * NY, NY)) * NC + core


def split(e):
    return lax.div(e, NY * NC), lax.rem(lax.div(e, NC), NY), lax.rem(e, NC)


def owner_of(e, z, t):
    x, y, _ = split(e)
    return ell_index(x + t, y + t + lax.div(z, NC), lax.rem(z, NC))


def kernel(
    owners_ref, counts_ref, shells_ref, start_ref, scale_ref, shift_ref, damp_ref, out_ref,
    order, coef, coef_v, stage_start, stage_shells, got_start, got_shells, tables, sums,
    coef_sem, send_start, recv_start, send_shells, recv_shells, send_out, recv_out,
):
    e, z = lax.axis_index("ell"), lax.axis_index("rad")
    x, y, core = split(e)

    def device(to_e, to_z):
        return {"ell": to_e, "rad": to_z}

    barrier = pltpu.get_barrier_semaphore()
    for d in range(1, NZ):
        pl.semaphore_signal(barrier, inc=1, device_id=device(e, lax.rem(z + d, NZ)), device_id_type=MESH)
    has_self = z == core
    for t in range(PER):
        for jy in range(NY):
            for c in range(NC):
                src_e, src_z = ell_index(x - t, y - t - jy, c), jy * NC + core
                if t == 0 and jy == 0:

                    @pl.when(jnp.logical_not(jnp.logical_and(src_e == e, src_z == z)))
                    def _():
                        pl.semaphore_signal(barrier, inc=1, device_id=device(src_e, src_z), device_id_type=MESH)
                else:
                    pl.semaphore_signal(barrier, inc=1, device_id=device(src_e, src_z), device_id_type=MESH)

    words = [jnp.int32(0)] * (GROUPS // 4)
    for p in range(GROUPS):
        o = owners_ref[p]
        high, low = o >> 2, o & 3
        value = jnp.where(low == 0, p, jnp.where(low == 1, p << 8, jnp.where(low == 2, p << 16, p << 24)))
        for k in range(GROUPS // 4):
            words[k] = words[k] + jnp.where(high == k, value, 0)
    for k in range(GROUPS // 4):
        for b in range(4):
            order[4 * k + b] = (words[k] >> (8 * b)) & 31

    coef_v[...] = jnp.zeros_like(coef_v)
    stage_start[...] = jnp.zeros_like(stage_start)
    mine = [order[owner_of(e, z, t)] for t in range(PER)]
    for t in range(PER):
        for i, ref in enumerate((scale_ref, shift_ref, damp_ref)):
            coef_v[i, pl.ds(t, 1), :] = ref[pl.ds(mine[t], 1), :]
    to_scalar = pltpu.make_async_copy(coef_v, coef, coef_sem)
    to_scalar.start()

    for d in range(NZ):
        to_z = lax.rem(z + d, NZ)
        for t in range(PER):
            p = order[owner_of(e, to_z, t)]
            row = start_ref[pl.ds(p, 1), :]
            if d == 0:
                got_start[pl.ds(z * 8 + t, 1), :] = row
                got_shells[t, pl.ds(pl.multiple_of(z * BLOCK, BLOCK), BLOCK), :] = shells_ref[p]
            else:
                stage_start[d - 1, pl.ds(t, 1), :] = row
                stage_shells[d - 1, t] = shells_ref[p]

    pl.semaphore_wait(barrier, NZ - 1 + GROUPS - has_self.astype(jnp.int32))

    def start_copy(d):
        return pltpu.make_async_remote_copy(
            src_ref=stage_start.at[d - 1],
            dst_ref=got_start.at[pl.ds(pl.multiple_of(z * 8, 8), 8)],
            send_sem=send_start.at[d - 1],
            recv_sem=recv_start.at[d - 1],
            device_id=device(e, lax.rem(z + d, NZ)),
            device_id_type=MESH,
        )

    def shell_copy(t, d):
        return pltpu.make_async_remote_copy(
            src_ref=stage_shells.at[d - 1, t],
            dst_ref=got_shells.at[t, pl.ds(pl.multiple_of(z * BLOCK, BLOCK), BLOCK)],
            send_sem=send_shells.at[d - 1, t],
            recv_sem=recv_shells.at[d - 1, t],
            device_id=device(e, lax.rem(z + d, NZ)),
            device_id_type=MESH,
        )

    far_first = (4, 3, 5, 2, 6, 1, 7)
    for d in far_first:
        start_copy(d).start()
    for t in range(PER):
        for d in far_first:
            shell_copy(t, d).start()

    for d in range(1, NZ):
        start_copy(d).wait_recv()
    to_scalar.wait()

    index = lax.broadcasted_iota(jnp.int32, (NZ, BLOCK), 0) * BLOCK + lax.broadcasted_iota(jnp.int32, (NZ, BLOCK), 1)
    nodes = jnp.cos(jnp.pi * (2.0 * index.astype(jnp.float32) + 1.0) / (2.0 * R))

    def eight(block, carry):
        carry = list(carry)
        for u in range(8):
            n = block * 8 + u
            for t in range(PER):
                before, now = carry[t]
                tables[t, block, pl.ds(u, NZ, stride=8), :] = now
                after = coef[0, t, n] * (nodes + coef[1, t, n]) * now - coef[2, t, n] * before
                carry[t] = (now, after)
        return tuple(carry)

    first = tuple((jnp.zeros((NZ, BLOCK), jnp.float32), got_start[pl.ds(t, NZ, stride=8), :]) for t in range(PER))
    lax.fori_loop(0, NDEG // 8, eight, first)

    def out_copy(t, d, here=False):
        to_z = lax.rem(z + d, NZ)
        src = sums.at[t, pl.ds(pl.multiple_of(to_z * SHARE, SHARE), SHARE)]
        if here:
            return pltpu.make_async_copy(src, out_ref.at[e], recv_out.at[e])
        return pltpu.make_async_remote_copy(
            src_ref=src,
            dst_ref=out_ref.at[e],
            send_sem=send_out.at[t, d],
            recv_sem=recv_out.at[e],
            device_id=device(owner_of(e, z, t), to_z),
            device_id_type=MESH,
        )

    for t in range(PER):
        for d in range(1, NZ):
            shell_copy(t, d).wait_recv()
        live = counts_ref[mine[t]]
        rows = 128

        def dots(step, _):
            base = step * (rows // 8)
            degree = lax.broadcasted_iota(jnp.int32, (rows, BLOCK), 0) + step * rows
            keep = degree < live
            left = jnp.concatenate(
                [
                    jnp.where(keep, tables[t, pl.ds(base, rows // 8), pl.ds(s * 8, 8), :].reshape(rows, BLOCK), 0.0).astype(jnp.bfloat16)
                    for s in range(NZ)
                ],
                axis=1,
            )
            total = jnp.dot(left, got_shells[t], preferred_element_type=jnp.float32)
            sums[t, pl.ds(pl.multiple_of(step * rows, rows), rows), :] = total.astype(jnp.bfloat16)
            return 0

        lax.fori_loop(0, NDEG // rows, dots, 0)
        for d in range(NZ):
            if t == 0 and d == 0:
                pl.when(has_self)(lambda: out_copy(0, 0, here=True).start())
                pl.when(jnp.logical_not(has_self))(lambda: out_copy(0, 0).start())
            else:
                out_copy(t, d).start()

    for t in range(PER):
        for jy in range(NY):
            for c in range(NC):
                slot = ell_index(x - t, y - t - jy, c)
                pltpu.make_async_copy(out_ref.at[slot], out_ref.at[slot], recv_out.at[slot]).wait()
    for d in far_first:
        start_copy(d).wait_send()
    for t in range(PER):
        for d in far_first:
            shell_copy(t, d).wait_send()
        for d in range(NZ):
            if t == 0 and d == 0:
                pl.when(jnp.logical_not(has_self))(lambda: out_copy(0, 0).wait_send())
            else:
                out_copy(t, d).wait_send()


def body(shells, start_values, rec_scale, rec_shift, rec_damp, degree_counts, owners):
    vmem = pl.BlockSpec(memory_space=pltpu.VMEM)
    smem = pl.BlockSpec(memory_space=pltpu.SMEM)
    dma = pltpu.SemaphoreType.DMA
    arrived = pl.pallas_call(
        kernel,
        out_shape=jax.ShapeDtypeStruct((GROUPS, SHARE, C), jnp.bfloat16),
        in_specs=[smem, smem, vmem, vmem, vmem, vmem, vmem],
        out_specs=vmem,
        scratch_shapes=[
            pltpu.SMEM((GROUPS,), jnp.int32),
            pltpu.SMEM((3, 8, NDEG), jnp.float32),
            pltpu.VMEM((3, 8, NDEG), jnp.float32),
            pltpu.VMEM((NZ - 1, 8, BLOCK), jnp.float32),
            pltpu.VMEM((NZ - 1, PER, BLOCK, C), jnp.bfloat16),
            pltpu.VMEM((NZ * 8, BLOCK), jnp.float32),
            pltpu.VMEM((PER, R, C), jnp.bfloat16),
            pltpu.VMEM((PER, NDEG // 8, NZ * 8, BLOCK), jnp.float32),
            pltpu.VMEM((PER, NDEG, C), jnp.bfloat16),
            dma,
            dma((NZ - 1,)),
            dma((NZ - 1,)),
            dma((NZ - 1, PER)),
            dma((NZ - 1, PER)),
            dma((PER, NZ)),
            dma((GROUPS,)),
        ],
        compiler_params=pltpu.CompilerParams(
            collective_id=0, has_side_effects=True, vmem_limit_bytes=40 * 2**20
        ),
        name="transform",
    )(owners, degree_counts, shells, start_values, rec_scale, rec_shift, rec_damp)
    return arrived.astype(jnp.float32)


def solution(mesh):
    return jax.shard_map(
        body,
        mesh=mesh,
        in_specs=(
            P("ell", "rad", None),
            P("ell", "rad"),
            P("ell", None),
            P("ell", None),
            P("ell", None),
            P("ell"),
            P("ell"),
        ),
        out_specs=P("ell", "rad", None),
        check_vma=False,
    )
```

```python
import jax
import jax.numpy as jnp
from jax import lax
from jax.experimental import pallas as pl
from jax.experimental.pallas import tpu as pltpu
from jax.sharding import PartitionSpec as P

MESH = pl.DeviceIdType.MESH
R = 1024
NDEG = 512
C = 128
NX, NY, NC, NZ = 4, 4, 2, 8
GROUPS = NX * NY * NC
PER = GROUPS // NZ
BLOCK = R // NZ
SHARE = NDEG // NZ


def ell_index(x, y, core):
    return (lax.rem(x + 2 * NX, NX) * NY + lax.rem(y + 2 * NY, NY)) * NC + core


def split(e):
    return lax.div(e, NY * NC), lax.rem(lax.div(e, NC), NY), lax.rem(e, NC)


def owner_of(e, z, t):
    x, y, _ = split(e)
    return ell_index(x + t, y + t + lax.div(z, NC), lax.rem(z, NC))


def kernel(
    owners_hbm, counts_hbm, shells_hbm, start_hbm, scale_hbm, shift_hbm, damp_hbm, out_ref,
    owners_ref, counts_ref, shells_ref, start_ref, scale_ref, shift_ref, damp_ref, load_sem,
    order, coef, coef_v, stage_start, stage_shells, got_start, got_shells, tables, sums,
    coef_sem, send_start, recv_start, send_shells, recv_shells, send_out, recv_out,
):
    e, z = lax.axis_index("ell"), lax.axis_index("rad")
    x, y, core = split(e)

    def device(to_e, to_z):
        return {"ell": to_e, "rad": to_z}

    parts = 4
    loads = [
        pltpu.make_async_copy(src, dst, load_sem.at[i])
        for i, (src, dst) in enumerate(
            (
                (owners_hbm, owners_ref),
                (start_hbm, start_ref),
                (counts_hbm, counts_ref),
                (scale_hbm, scale_ref),
                (shift_hbm, shift_ref),
                (damp_hbm, damp_ref),
            )
        )
    ]
    part = GROUPS // parts
    loads += [
        pltpu.make_async_copy(
            shells_hbm.at[pl.ds(i * part, part)], shells_ref.at[pl.ds(i * part, part)], load_sem.at[6 + i]
        )
        for i in range(parts)
    ]
    for load in loads:
        load.start()

    barrier = pltpu.get_barrier_semaphore()
    for d in range(1, NZ):
        pl.semaphore_signal(barrier, inc=1, device_id=device(e, lax.rem(z + d, NZ)), device_id_type=MESH)
    has_self = z == core
    for t in range(PER):
        for jy in range(NY):
            for c in range(NC):
                src_e, src_z = ell_index(x - t, y - t - jy, c), jy * NC + core
                if t == 0 and jy == 0:

                    @pl.when(jnp.logical_not(jnp.logical_and(src_e == e, src_z == z)))
                    def _():
                        pl.semaphore_signal(barrier, inc=1, device_id=device(src_e, src_z), device_id_type=MESH)
                else:
                    pl.semaphore_signal(barrier, inc=1, device_id=device(src_e, src_z), device_id_type=MESH)

    loads[0].wait()
    words = [jnp.int32(0)] * (GROUPS // 4)
    for p in range(GROUPS):
        o = owners_ref[p]
        high, low = o >> 2, o & 3
        value = jnp.where(low == 0, p, jnp.where(low == 1, p << 8, jnp.where(low == 2, p << 16, p << 24)))
        for k in range(GROUPS // 4):
            words[k] = words[k] + jnp.where(high == k, value, 0)
    for k in range(GROUPS // 4):
        for b in range(4):
            order[4 * k + b] = (words[k] >> (8 * b)) & 31

    for load in loads[1:6]:
        load.wait()
    coef_v[...] = jnp.zeros_like(coef_v)
    stage_start[...] = jnp.zeros_like(stage_start)
    mine = [order[owner_of(e, z, t)] for t in range(PER)]
    for t in range(PER):
        for i, ref in enumerate((scale_ref, shift_ref, damp_ref)):
            coef_v[i, pl.ds(t, 1), :] = ref[pl.ds(mine[t], 1), :]
    to_scalar = pltpu.make_async_copy(coef_v, coef, coef_sem)
    to_scalar.start()

    for load in loads[6:]:
        load.wait()
    for d in range(NZ):
        to_z = lax.rem(z + d, NZ)
        for t in range(PER):
            p = order[owner_of(e, to_z, t)]
            row = start_ref[pl.ds(p, 1), :]
            if d == 0:
                got_start[pl.ds(z * 8 + t, 1), :] = row
                got_shells[t, pl.ds(pl.multiple_of(z * BLOCK, BLOCK), BLOCK), :] = shells_ref[p]
            else:
                stage_start[d - 1, pl.ds(t, 1), :] = row
                stage_shells[d - 1, t] = shells_ref[p]

    pl.semaphore_wait(barrier, NZ - 1 + GROUPS - has_self.astype(jnp.int32))

    def start_copy(d):
        return pltpu.make_async_remote_copy(
            src_ref=stage_start.at[d - 1],
            dst_ref=got_start.at[pl.ds(pl.multiple_of(z * 8, 8), 8)],
            send_sem=send_start.at[d - 1],
            recv_sem=recv_start.at[d - 1],
            device_id=device(e, lax.rem(z + d, NZ)),
            device_id_type=MESH,
        )

    def shell_copy(t, d):
        return pltpu.make_async_remote_copy(
            src_ref=stage_shells.at[d - 1, t],
            dst_ref=got_shells.at[t, pl.ds(pl.multiple_of(z * BLOCK, BLOCK), BLOCK)],
            send_sem=send_shells.at[d - 1, t],
            recv_sem=recv_shells.at[d - 1, t],
            device_id=device(e, lax.rem(z + d, NZ)),
            device_id_type=MESH,
        )

    far_first = (4, 3, 5, 2, 6, 1, 7)
    for d in far_first:
        start_copy(d).start()
    for t in range(PER):
        for d in far_first:
            shell_copy(t, d).start()

    for d in range(1, NZ):
        start_copy(d).wait_recv()
    to_scalar.wait()

    index = lax.broadcasted_iota(jnp.int32, (NZ, BLOCK), 0) * BLOCK + lax.broadcasted_iota(jnp.int32, (NZ, BLOCK), 1)
    nodes = jnp.cos(jnp.pi * (2.0 * index.astype(jnp.float32) + 1.0) / (2.0 * R))

    def eight(block, carry):
        carry = list(carry)
        for u in range(8):
            n = block * 8 + u
            for t in range(PER):
                before, now = carry[t]
                tables[t, block, pl.ds(u, NZ, stride=8), :] = now
                after = coef[0, t, n] * (nodes + coef[1, t, n]) * now - coef[2, t, n] * before
                carry[t] = (now, after)
        return tuple(carry)

    first = tuple((jnp.zeros((NZ, BLOCK), jnp.float32), got_start[pl.ds(t, NZ, stride=8), :]) for t in range(PER))
    lax.fori_loop(0, NDEG // 8, eight, first)

    def out_copy(t, d, here=False):
        to_z = lax.rem(z + d, NZ)
        src = sums.at[t, pl.ds(pl.multiple_of(to_z * SHARE, SHARE), SHARE)]
        if here:
            return pltpu.make_async_copy(src, out_ref.at[e], recv_out.at[e])
        return pltpu.make_async_remote_copy(
            src_ref=src,
            dst_ref=out_ref.at[e],
            send_sem=send_out.at[t, d],
            recv_sem=recv_out.at[e],
            device_id=device(owner_of(e, z, t), to_z),
            device_id_type=MESH,
        )

    for t in range(PER):
        for d in range(1, NZ):
            shell_copy(t, d).wait_recv()
        live = counts_ref[mine[t]]
        rows = 128

        def dots(step, _):
            base = step * (rows // 8)
            degree = lax.broadcasted_iota(jnp.int32, (rows, BLOCK), 0) + step * rows
            keep = degree < live
            left = jnp.concatenate(
                [
                    jnp.where(keep, tables[t, pl.ds(base, rows // 8), pl.ds(s * 8, 8), :].reshape(rows, BLOCK), 0.0).astype(jnp.bfloat16)
                    for s in range(NZ)
                ],
                axis=1,
            )
            total = jnp.dot(left, got_shells[t], preferred_element_type=jnp.float32)
            sums[t, pl.ds(pl.multiple_of(step * rows, rows), rows), :] = total.astype(jnp.bfloat16)
            return 0

        lax.fori_loop(0, NDEG // rows, dots, 0)
        for d in range(NZ):
            if t == 0 and d == 0:
                pl.when(has_self)(lambda: out_copy(0, 0, here=True).start())
                pl.when(jnp.logical_not(has_self))(lambda: out_copy(0, 0).start())
            else:
                out_copy(t, d).start()

    for t in range(PER):
        for jy in range(NY):
            for c in range(NC):
                slot = ell_index(x - t, y - t - jy, c)
                pltpu.make_async_copy(out_ref.at[slot], out_ref.at[slot], recv_out.at[slot]).wait()
    for d in far_first:
        start_copy(d).wait_send()
    for t in range(PER):
        for d in far_first:
            shell_copy(t, d).wait_send()
        for d in range(NZ):
            if t == 0 and d == 0:
                pl.when(jnp.logical_not(has_self))(lambda: out_copy(0, 0).wait_send())
            else:
                out_copy(t, d).wait_send()


def body(shells, start_values, rec_scale, rec_shift, rec_damp, degree_counts, owners):
    hbm = pl.BlockSpec(memory_space=pltpu.HBM)
    dma = pltpu.SemaphoreType.DMA
    arrived = pl.pallas_call(
        kernel,
        out_shape=jax.ShapeDtypeStruct((GROUPS, SHARE, C), jnp.bfloat16),
        in_specs=[hbm] * 7,
        out_specs=hbm,
        scratch_shapes=[
            pltpu.SMEM((GROUPS,), jnp.int32),
            pltpu.SMEM((GROUPS,), jnp.int32),
            pltpu.VMEM((GROUPS, BLOCK, C), jnp.bfloat16),
            pltpu.VMEM((GROUPS, BLOCK), jnp.float32),
            pltpu.VMEM((GROUPS, NDEG), jnp.float32),
            pltpu.VMEM((GROUPS, NDEG), jnp.float32),
            pltpu.VMEM((GROUPS, NDEG), jnp.float32),
            dma((10,)),
            pltpu.SMEM((GROUPS,), jnp.int32),
            pltpu.SMEM((3, 8, NDEG), jnp.float32),
            pltpu.VMEM((3, 8, NDEG), jnp.float32),
            pltpu.VMEM((NZ - 1, 8, BLOCK), jnp.float32),
            pltpu.VMEM((NZ - 1, PER, BLOCK, C), jnp.bfloat16),
            pltpu.VMEM((NZ * 8, BLOCK), jnp.float32),
            pltpu.VMEM((PER, R, C), jnp.bfloat16),
            pltpu.VMEM((PER, NDEG // 8, NZ * 8, BLOCK), jnp.float32),
            pltpu.VMEM((PER, NDEG, C), jnp.bfloat16),
            dma,
            dma((NZ - 1,)),
            dma((NZ - 1,)),
            dma((NZ - 1, PER)),
            dma((NZ - 1, PER)),
            dma((PER, NZ)),
            dma((GROUPS,)),
        ],
        compiler_params=pltpu.CompilerParams(
            collective_id=0, has_side_effects=True, vmem_limit_bytes=62 * 2**20 - 2**18
        ),
        name="transform",
    )(owners, degree_counts, shells, start_values, rec_scale, rec_shift, rec_damp)
    return arrived.astype(jnp.float32)


def solution(mesh):
    return jax.shard_map(
        body,
        mesh=mesh,
        in_specs=(
            P("ell", "rad", None),
            P("ell", "rad"),
            P("ell", None),
            P("ell", None),
            P("ell", None),
            P("ell"),
            P("ell"),
        ),
        out_specs=P("ell", "rad", None),
        check_vma=False,
    )
```

```python
import jax
import jax.numpy as jnp
from jax import lax
from jax.experimental import pallas as pl
from jax.experimental.pallas import tpu as pltpu
from jax.sharding import PartitionSpec as P

MESH = pl.DeviceIdType.MESH
R = 1024
NDEG = 512
C = 128
NX, NY, NC, NZ = 4, 4, 2, 8
GROUPS = NX * NY * NC
PER = GROUPS // NZ
BLOCK = R // NZ
SHARE = NDEG // NZ


def ell_index(x, y, core):
    return (lax.rem(x + 2 * NX, NX) * NY + lax.rem(y + 2 * NY, NY)) * NC + core


def split(e):
    return lax.div(e, NY * NC), lax.rem(lax.div(e, NC), NY), lax.rem(e, NC)


def owner_of(e, z, t):
    x, y, core = split(e)
    return ell_index(x + t, y + t + lax.div(z, NC), lax.rem(core + z, NC))


def group_of(o, z, t):
    x, y, core = split(o)
    return ell_index(x - t, y - t - lax.div(z, NC), lax.rem(core + z, NC))


def kernel(
    owners_hbm, counts_hbm, shells_hbm, start_hbm, scale_hbm, shift_hbm, damp_hbm, out_ref,
    owners_ref, counts_ref, shells_ref, start_ref, scale_ref, shift_ref, damp_ref, load_sem,
    order, coef, coef_v, stage_start, stage_shells, got_start, got_shells, tables, rounded, sums, hopped,
    coef_sem, send_start, recv_start, send_shells, recv_shells, send_hop, recv_hop, send_out, recv_out,
):
    e, z = lax.axis_index("ell"), lax.axis_index("rad")

    def device(to_e, to_z):
        return {"ell": to_e, "rad": to_z}

    parts = 4
    loads = [
        pltpu.make_async_copy(src, dst, load_sem.at[i])
        for i, (src, dst) in enumerate(
            (
                (owners_hbm, owners_ref),
                (start_hbm, start_ref),
                (counts_hbm, counts_ref),
                (scale_hbm, scale_ref),
                (shift_hbm, shift_ref),
                (damp_hbm, damp_ref),
            )
        )
    ]
    part = GROUPS // parts
    loads += [
        pltpu.make_async_copy(
            shells_hbm.at[pl.ds(i * part, part)], shells_ref.at[pl.ds(i * part, part)], load_sem.at[6 + i]
        )
        for i in range(parts)
    ]
    for load in loads:
        load.start()

    barrier = pltpu.get_barrier_semaphore()
    for d in range(1, NZ):
        pl.semaphore_signal(barrier, inc=1, device_id=device(e, lax.rem(z + d, NZ)), device_id_type=MESH)
    stays = z == 0
    for t in range(PER):

        def greet(t=t):
            pl.semaphore_signal(barrier, inc=1, device_id=device(group_of(e, z, t), z), device_id_type=MESH)

        if t == 0:
            pl.when(jnp.logical_not(stays))(greet)
        else:
            greet()

    loads[0].wait()
    words = [jnp.int32(0)] * (GROUPS // 4)
    for p in range(GROUPS):
        o = owners_ref[p]
        high, low = o >> 2, o & 3
        value = jnp.where(low == 0, p, jnp.where(low == 1, p << 8, jnp.where(low == 2, p << 16, p << 24)))
        for k in range(GROUPS // 4):
            words[k] = words[k] + jnp.where(high == k, value, 0)
    for k in range(GROUPS // 4):
        for b in range(4):
            order[4 * k + b] = (words[k] >> (8 * b)) & 31

    def start_copy(d):
        return pltpu.make_async_remote_copy(
            src_ref=stage_start.at[d - 1],
            dst_ref=got_start.at[pl.ds(pl.multiple_of(z * 8, 8), 8)],
            send_sem=send_start.at[d - 1],
            recv_sem=recv_start.at[d - 1],
            device_id=device(e, lax.rem(z + d, NZ)),
            device_id_type=MESH,
        )

    def shell_copy(t, d):
        return pltpu.make_async_remote_copy(
            src_ref=stage_shells.at[d - 1, t],
            dst_ref=got_shells.at[t, pl.ds(pl.multiple_of(z * BLOCK, BLOCK), BLOCK)],
            send_sem=send_shells.at[d - 1, t],
            recv_sem=recv_shells.at[d - 1, t],
            device_id=device(e, lax.rem(z + d, NZ)),
            device_id_type=MESH,
        )

    far_first = (4, 3, 5, 2, 6, 1, 7)
    loads[1].wait()
    stage_start[...] = jnp.zeros_like(stage_start)
    to = [[order[owner_of(e, lax.rem(z + d, NZ), t)] for t in range(PER)] for d in range(NZ)]
    for d in range(1, NZ):
        for t in range(PER):
            stage_start[d - 1, pl.ds(t, 1), :] = start_ref[pl.ds(to[d][t], 1), :]
    for load in loads[6:]:
        load.wait()
    for d in far_first:
        stage_shells[d - 1, 0] = shells_ref[to[d][0]]
    pl.semaphore_wait(barrier, NZ - 1 + PER - stays.astype(jnp.int32))
    for d in far_first:
        shell_copy(0, d).start()
        start_copy(d).start()
    for t in range(1, PER):
        for d in far_first:
            stage_shells[d - 1, t] = shells_ref[to[d][t]]
            shell_copy(t, d).start()

    mine = to[0]
    for t in range(PER):
        got_start[pl.ds(z * 8 + t, 1), :] = start_ref[pl.ds(mine[t], 1), :]
        got_shells[t, pl.ds(pl.multiple_of(z * BLOCK, BLOCK), BLOCK), :] = shells_ref[mine[t]]

    for load in loads[2:6]:
        load.wait()
    coef_v[...] = jnp.zeros_like(coef_v)
    for t in range(PER):
        for i, ref in enumerate((scale_ref, shift_ref, damp_ref)):
            coef_v[i, pl.ds(t, 1), :] = ref[pl.ds(mine[t], 1), :]
    to_scalar = pltpu.make_async_copy(coef_v, coef, coef_sem)
    to_scalar.start()

    for d in range(1, NZ):
        start_copy(d).wait_recv()
    to_scalar.wait()

    index = lax.broadcasted_iota(jnp.int32, (NZ, BLOCK), 0) * BLOCK + lax.broadcasted_iota(jnp.int32, (NZ, BLOCK), 1)
    nodes = jnp.cos(jnp.pi * (2.0 * index.astype(jnp.float32) + 1.0) / (2.0 * R))

    def eight(block, carry):
        carry = list(carry)
        for u in range(8):
            n = block * 8 + u
            for t in range(PER):
                before, now = carry[t]
                tables[t, block, pl.ds(u, NZ, stride=8), :] = now
                after = coef[0, t, n] * (nodes + coef[1, t, n]) * now - coef[2, t, n] * before
                carry[t] = (now, after)
        return tuple(carry)

    first = tuple((jnp.zeros((NZ, BLOCK), jnp.float32), got_start[pl.ds(t, NZ, stride=8), :]) for t in range(PER))
    lax.fori_loop(0, NDEG // 8, eight, first)

    def hop_copy(t):
        return pltpu.make_async_remote_copy(
            src_ref=sums.at[t],
            dst_ref=hopped.at[t],
            send_sem=send_hop.at[t],
            recv_sem=recv_hop.at[t],
            device_id=device(owner_of(e, z, t), z),
            device_id_type=MESH,
        )

    def hop_here(t):
        return pltpu.make_async_copy(sums.at[t], hopped.at[t], recv_hop.at[t])

    def out_copy(t, d):
        to_z = lax.rem(z + d, NZ)
        slot = group_of(e, z, t)
        src = hopped.at[t, pl.ds(pl.multiple_of(to_z * SHARE, SHARE), SHARE)]
        if d == 0:
            return pltpu.make_async_copy(src, out_ref.at[slot], recv_out.at[slot])
        return pltpu.make_async_remote_copy(
            src_ref=src,
            dst_ref=out_ref.at[slot],
            send_sem=send_out.at[t, d - 1],
            recv_sem=recv_out.at[slot],
            device_id=device(e, to_z),
            device_id_type=MESH,
        )

    def forward(t):
        hop_here(t).wait()
        for d in (*far_first, 0):
            out_copy(t, d).start()

    rows = 128
    for t in range(PER):
        live = counts_ref[mine[t]]

        def round_rows(step, _):
            degree = lax.broadcasted_iota(jnp.int32, (rows, BLOCK), 0) + step * rows
            for s in range(NZ):
                tall = tables[t, pl.ds(step * (rows // 8), rows // 8), pl.ds(s * 8, 8), :].reshape(rows, BLOCK)
                rounded[t, pl.ds(pl.multiple_of(step * rows, rows), rows), pl.ds(s * BLOCK, BLOCK)] = jnp.where(
                    degree < live, tall, 0.0
                ).astype(jnp.bfloat16)
            return 0

        lax.fori_loop(0, NDEG // rows, round_rows, 0)

    for t in range(PER):
        for d in range(1, NZ):
            shell_copy(t, d).wait_recv()
        total = jnp.dot(rounded[t], got_shells[t], preferred_element_type=jnp.float32)
        sums[t] = total.astype(jnp.bfloat16)
        if t == 0:
            pl.when(stays)(lambda: hop_here(0).start())
            pl.when(jnp.logical_not(stays))(lambda: hop_copy(0).start())
        else:
            hop_copy(t).start()
            forward(t - 1)
    forward(PER - 1)

    for j in range(NZ):
        for t in range(PER):
            slot = group_of(e, j, t)
            pltpu.make_async_copy(out_ref.at[slot], out_ref.at[slot], recv_out.at[slot]).wait()
    pl.when(jnp.logical_not(stays))(lambda: hop_copy(0).wait_send())
    for t in range(1, PER):
        hop_copy(t).wait_send()
    for d in far_first:
        start_copy(d).wait_send()
    for t in range(PER):
        for d in far_first:
            shell_copy(t, d).wait_send()
            out_copy(t, d).wait_send()


def body(shells, start_values, rec_scale, rec_shift, rec_damp, degree_counts, owners):
    hbm = pl.BlockSpec(memory_space=pltpu.HBM)
    dma = pltpu.SemaphoreType.DMA
    arrived = pl.pallas_call(
        kernel,
        out_shape=jax.ShapeDtypeStruct((GROUPS, SHARE, C), jnp.bfloat16),
        in_specs=[hbm] * 7,
        out_specs=hbm,
        scratch_shapes=[
            pltpu.SMEM((GROUPS,), jnp.int32),
            pltpu.SMEM((GROUPS,), jnp.int32),
            pltpu.VMEM((GROUPS, BLOCK, C), jnp.bfloat16),
            pltpu.VMEM((GROUPS, BLOCK), jnp.float32),
            pltpu.VMEM((GROUPS, NDEG), jnp.float32),
            pltpu.VMEM((GROUPS, NDEG), jnp.float32),
            pltpu.VMEM((GROUPS, NDEG), jnp.float32),
            dma((10,)),
            pltpu.SMEM((GROUPS,), jnp.int32),
            pltpu.SMEM((3, 8, NDEG), jnp.float32),
            pltpu.VMEM((3, 8, NDEG), jnp.float32),
            pltpu.VMEM((NZ - 1, 8, BLOCK), jnp.float32),
            pltpu.VMEM((NZ - 1, PER, BLOCK, C), jnp.bfloat16),
            pltpu.VMEM((NZ * 8, BLOCK), jnp.float32),
            pltpu.VMEM((PER, R, C), jnp.bfloat16),
            pltpu.VMEM((PER, NDEG // 8, NZ * 8, BLOCK), jnp.float32),
            pltpu.VMEM((PER, NDEG, R), jnp.bfloat16),
            pltpu.VMEM((PER, NDEG, C), jnp.bfloat16),
            pltpu.VMEM((PER, NDEG, C), jnp.bfloat16),
            dma,
            dma((NZ - 1,)),
            dma((NZ - 1,)),
            dma((NZ - 1, PER)),
            dma((NZ - 1, PER)),
            dma((PER,)),
            dma((PER,)),
            dma((PER, NZ - 1)),
            dma((GROUPS,)),
        ],
        compiler_params=pltpu.CompilerParams(
            collective_id=0, has_side_effects=True, vmem_limit_bytes=62 * 2**20 - 2**18
        ),
        name="transform",
    )(owners, degree_counts, shells, start_values, rec_scale, rec_shift, rec_damp)
    return arrived.astype(jnp.float32)


def solution(mesh):
    return jax.shard_map(
        body,
        mesh=mesh,
        in_specs=(
            P("ell", "rad", None),
            P("ell", "rad"),
            P("ell", None),
            P("ell", None),
            P("ell", None),
            P("ell"),
            P("ell"),
        ),
        out_specs=P("ell", "rad", None),
        check_vma=False,
    )
```

```python
import jax
import jax.numpy as jnp
from jax import lax
from jax.experimental import pallas as pl
from jax.experimental.pallas import tpu as pltpu
from jax.sharding import PartitionSpec as P

MESH = pl.DeviceIdType.MESH
R = 1024
NDEG = 512
C = 128
NX, NY, NC, NZ = 4, 4, 2, 8
GROUPS = NX * NY * NC
PER = GROUPS // NZ
BLOCK = R // NZ
SHARE = NDEG // NZ
STEPS = (2, 3, 1, 0)
HOME = 3


def ell_index(x, y, core):
    return (lax.rem(x + 2 * NX, NX) * NY + lax.rem(y + 2 * NY, NY)) * NC + core


def split(e):
    return lax.div(e, NY * NC), lax.rem(lax.div(e, NC), NY), lax.rem(e, NC)


def owner_of(e, z, t):
    x, y, core = split(e)
    way = 1 - 2 * core
    return ell_index(x + way * STEPS[t], y + way * (STEPS[t] + lax.div(z, NC)), lax.rem(core + z, NC))


def group_of(o, z, t):
    x, y, core = split(o)
    core = lax.rem(core + z, NC)
    way = 1 - 2 * core
    return ell_index(x - way * STEPS[t], y - way * (STEPS[t] + lax.div(z, NC)), core)


def kernel(
    owners_hbm, counts_hbm, shells_hbm, start_hbm, scale_hbm, shift_hbm, damp_hbm, out_ref,
    owners_ref, counts_ref, shells_ref, start_ref, scale_ref, shift_ref, damp_ref, load_sem,
    order, coef, coef_v, stage_start, stage_shells, got_start, got_shells, tables, rounded, sums, hopped,
    coef_sem, send_start, recv_start, send_shells, recv_shells, send_hop, recv_hop, send_out, recv_out,
):
    e, z = lax.axis_index("ell"), lax.axis_index("rad")

    def device(to_e, to_z):
        return {"ell": to_e, "rad": to_z}

    parts = 4
    loads = [
        pltpu.make_async_copy(src, dst, load_sem.at[i])
        for i, (src, dst) in enumerate(
            (
                (owners_hbm, owners_ref),
                (start_hbm, start_ref),
                (counts_hbm, counts_ref),
                (scale_hbm, scale_ref),
                (shift_hbm, shift_ref),
                (damp_hbm, damp_ref),
            )
        )
    ]
    part = GROUPS // parts
    loads += [
        pltpu.make_async_copy(
            shells_hbm.at[pl.ds(i * part, part)], shells_ref.at[pl.ds(i * part, part)], load_sem.at[6 + i]
        )
        for i in range(parts)
    ]
    for load in loads:
        load.start()

    barrier = pltpu.get_barrier_semaphore()
    for d in range(1, NZ):
        pl.semaphore_signal(barrier, inc=1, device_id=device(e, lax.rem(z + d, NZ)), device_id_type=MESH)
    stays = z == 0
    for t in range(PER):

        def greet(t=t):
            pl.semaphore_signal(barrier, inc=1, device_id=device(group_of(e, z, t), z), device_id_type=MESH)

        if t == HOME:
            pl.when(jnp.logical_not(stays))(greet)
        else:
            greet()

    loads[0].wait()
    words = [jnp.int32(0)] * (GROUPS // 4)
    for p in range(GROUPS):
        o = owners_ref[p]
        high, low = o >> 2, o & 3
        value = jnp.where(low == 0, p, jnp.where(low == 1, p << 8, jnp.where(low == 2, p << 16, p << 24)))
        for k in range(GROUPS // 4):
            words[k] = words[k] + jnp.where(high == k, value, 0)
    for k in range(GROUPS // 4):
        for b in range(4):
            order[4 * k + b] = (words[k] >> (8 * b)) & 31

    def start_copy(d):
        return pltpu.make_async_remote_copy(
            src_ref=stage_start.at[d - 1],
            dst_ref=got_start.at[pl.ds(pl.multiple_of(z * 8, 8), 8)],
            send_sem=send_start.at[d - 1],
            recv_sem=recv_start.at[d - 1],
            device_id=device(e, lax.rem(z + d, NZ)),
            device_id_type=MESH,
        )

    def shell_copy(t, d):
        return pltpu.make_async_remote_copy(
            src_ref=stage_shells.at[d - 1, t],
            dst_ref=got_shells.at[t, pl.ds(pl.multiple_of(z * BLOCK, BLOCK), BLOCK)],
            send_sem=send_shells.at[d - 1, t],
            recv_sem=recv_shells.at[d - 1, t],
            device_id=device(e, lax.rem(z + d, NZ)),
            device_id_type=MESH,
        )

    far_first = (4, 3, 5, 2, 6, 1, 7)
    loads[1].wait()
    stage_start[...] = jnp.zeros_like(stage_start)
    to = [[order[owner_of(e, lax.rem(z + d, NZ), t)] for t in range(PER)] for d in range(NZ)]
    for d in range(1, NZ):
        for t in range(PER):
            stage_start[d - 1, pl.ds(t, 1), :] = start_ref[pl.ds(to[d][t], 1), :]
    for load in loads[6:]:
        load.wait()
    for d in far_first:
        stage_shells[d - 1, 0] = shells_ref[to[d][0]]
    pl.semaphore_wait(barrier, NZ - 1 + PER - stays.astype(jnp.int32))
    def send(t):
        for d in far_first:
            shell_copy(t, d).start()

    for d in far_first:
        start_copy(d).start()
    send(0)
    for t in range(1, PER):
        for d in far_first:
            stage_shells[d - 1, t] = shells_ref[to[d][t]]
        if t == 1:
            send(1)

    mine = to[0]
    for t in range(PER):
        got_start[pl.ds(z * 8 + t, 1), :] = start_ref[pl.ds(mine[t], 1), :]
        got_shells[t, pl.ds(pl.multiple_of(z * BLOCK, BLOCK), BLOCK), :] = shells_ref[mine[t]]

    for load in loads[2:6]:
        load.wait()
    coef_v[...] = jnp.zeros_like(coef_v)
    for t in range(PER):
        for i, ref in enumerate((scale_ref, shift_ref, damp_ref)):
            coef_v[i, pl.ds(t, 1), :] = ref[pl.ds(mine[t], 1), :]
    to_scalar = pltpu.make_async_copy(coef_v, coef, coef_sem)
    to_scalar.start()

    for d in range(1, NZ):
        start_copy(d).wait_recv()
    to_scalar.wait()

    index = lax.broadcasted_iota(jnp.int32, (NZ, BLOCK), 0) * BLOCK + lax.broadcasted_iota(jnp.int32, (NZ, BLOCK), 1)
    nodes = jnp.cos(jnp.pi * (2.0 * index.astype(jnp.float32) + 1.0) / (2.0 * R))

    def eight(block, carry):
        carry = list(carry)
        for u in range(8):
            n = block * 8 + u
            for t in range(PER):
                before, now = carry[t]
                tables[t, block, pl.ds(u, NZ, stride=8), :] = now
                after = coef[0, t, n] * (nodes + coef[1, t, n]) * now - coef[2, t, n] * before
                carry[t] = (now, after)
        return tuple(carry)

    first = tuple((jnp.zeros((NZ, BLOCK), jnp.float32), got_start[pl.ds(t, NZ, stride=8), :]) for t in range(PER))
    lax.fori_loop(0, NDEG // 8, eight, first)

    def hop_copy(t):
        return pltpu.make_async_remote_copy(
            src_ref=sums.at[t],
            dst_ref=hopped.at[t],
            send_sem=send_hop.at[t],
            recv_sem=recv_hop.at[t],
            device_id=device(owner_of(e, z, t), z),
            device_id_type=MESH,
        )

    def hop_here(t):
        return pltpu.make_async_copy(sums.at[t], hopped.at[t], recv_hop.at[t])

    def out_copy(t, k, here=False):
        slot = group_of(e, z, t)
        src = hopped.at[t, pl.ds(k * SHARE, SHARE)]
        if here:
            return pltpu.make_async_copy(src, out_ref.at[slot], recv_out.at[slot])
        return pltpu.make_async_remote_copy(
            src_ref=src,
            dst_ref=out_ref.at[slot],
            send_sem=send_out.at[t, k],
            recv_sem=recv_out.at[slot],
            device_id=device(e, k),
            device_id_type=MESH,
        )

    def forward(t, planes):
        for k in planes:
            pl.when(z == k)(lambda k=k: out_copy(t, k, here=True).start())
            pl.when(z != k)(lambda k=k: out_copy(t, k).start())

    def hop_in(t):
        hop_here(t).wait()

    rows = 128
    for t in range(PER):
        live = counts_ref[mine[t]]

        def round_rows(step, _):
            degree = lax.broadcasted_iota(jnp.int32, (rows, BLOCK), 0) + step * rows
            for s in range(NZ):
                tall = tables[t, pl.ds(step * (rows // 8), rows // 8), pl.ds(s * 8, 8), :].reshape(rows, BLOCK)
                rounded[t, pl.ds(pl.multiple_of(step * rows, rows), rows), pl.ds(s * BLOCK, BLOCK)] = jnp.where(
                    degree < live, tall, 0.0
                ).astype(jnp.bfloat16)
            return 0

        lax.fori_loop(0, NDEG // rows, round_rows, 0)

    def work(t):
        for d in range(1, NZ):
            shell_copy(t, d).wait_recv()
        total = jnp.dot(rounded[t], got_shells[t], preferred_element_type=jnp.float32)
        sums[t] = total.astype(jnp.bfloat16)
        if t == HOME:
            pl.when(stays)(lambda: hop_here(HOME).start())
            pl.when(jnp.logical_not(stays))(lambda: hop_copy(HOME).start())
        else:
            hop_copy(t).start()

    send(2)
    work(0)
    work(1)
    send(3)
    hop_in(0)
    forward(0, (0, 1, 2, 3, 7, 6, 4, 5))
    work(2)
    hop_in(1)
    forward(1, (0, 1, 2, 3, 7, 6, 4, 5))
    work(3)
    hop_in(2)
    forward(2, (0, 1, 2, 3, 7, 6, 4, 5))
    hop_in(3)
    forward(3, (0, 1, 2, 3, 7, 6, 4, 5))

    for j in range(NZ):
        for t in range(PER):
            slot = group_of(e, j, t)
            pltpu.make_async_copy(out_ref.at[slot], out_ref.at[slot], recv_out.at[slot]).wait()
    pl.when(jnp.logical_not(stays))(lambda: hop_copy(HOME).wait_send())
    for t in range(PER):
        if t != HOME:
            hop_copy(t).wait_send()
    for d in far_first:
        start_copy(d).wait_send()
    for t in range(PER):
        for d in far_first:
            shell_copy(t, d).wait_send()
        for k in range(NZ):
            pl.when(z != k)(lambda t=t, k=k: out_copy(t, k).wait_send())


def body(shells, start_values, rec_scale, rec_shift, rec_damp, degree_counts, owners):
    hbm = pl.BlockSpec(memory_space=pltpu.HBM)
    dma = pltpu.SemaphoreType.DMA
    arrived = pl.pallas_call(
        kernel,
        out_shape=pltpu.VMEM((GROUPS, SHARE, C), jnp.bfloat16),
        in_specs=[hbm] * 7,
        out_specs=pl.BlockSpec(memory_space=pltpu.VMEM),
        scratch_shapes=[
            pltpu.SMEM((GROUPS,), jnp.int32),
            pltpu.SMEM((GROUPS,), jnp.int32),
            pltpu.VMEM((GROUPS, BLOCK, C), jnp.bfloat16),
            pltpu.VMEM((GROUPS, BLOCK), jnp.float32),
            pltpu.VMEM((GROUPS, NDEG), jnp.float32),
            pltpu.VMEM((GROUPS, NDEG), jnp.float32),
            pltpu.VMEM((GROUPS, NDEG), jnp.float32),
            dma((10,)),
            pltpu.SMEM((GROUPS,), jnp.int32),
            pltpu.SMEM((3, 8, NDEG), jnp.float32),
            pltpu.VMEM((3, 8, NDEG), jnp.float32),
            pltpu.VMEM((NZ - 1, 8, BLOCK), jnp.float32),
            pltpu.VMEM((NZ - 1, PER, BLOCK, C), jnp.bfloat16),
            pltpu.VMEM((NZ * 8, BLOCK), jnp.float32),
            pltpu.VMEM((PER, R, C), jnp.bfloat16),
            pltpu.VMEM((PER, NDEG // 8, NZ * 8, BLOCK), jnp.float32),
            pltpu.VMEM((PER, NDEG, R), jnp.bfloat16),
            pltpu.VMEM((PER, NDEG, C), jnp.bfloat16),
            pltpu.VMEM((PER, NDEG, C), jnp.bfloat16),
            dma,
            dma((NZ - 1,)),
            dma((NZ - 1,)),
            dma((NZ - 1, PER)),
            dma((NZ - 1, PER)),
            dma((PER,)),
            dma((PER,)),
            dma((PER, NZ)),
            dma((GROUPS,)),
        ],
        compiler_params=pltpu.CompilerParams(
            collective_id=0, has_side_effects=True, vmem_limit_bytes=40 * 2**20
        ),
        name="transform",
    )(
        *(
            pltpu.with_memory_space_constraint(a, pltpu.HBM)
            for a in (owners, degree_counts, shells, start_values, rec_scale, rec_shift, rec_damp)
        )
    )
    return arrived.astype(jnp.float32)


def solution(mesh):
    return jax.shard_map(
        body,
        mesh=mesh,
        in_specs=(
            P("ell", "rad", None),
            P("ell", "rad"),
            P("ell", None),
            P("ell", None),
            P("ell", None),
            P("ell"),
            P("ell"),
        ),
        out_specs=P("ell", "rad", None),
        check_vma=False,
    )
```

```python
import jax
import jax.numpy as jnp
from jax import lax
from jax.experimental import pallas as pl
from jax.experimental.pallas import tpu as pltpu
from jax.sharding import PartitionSpec as P

MESH = pl.DeviceIdType.MESH
R = 1024
NDEG = 512
C = 128
NX, NY, NC, NZ = 4, 4, 2, 8
GROUPS = NX * NY * NC
PER = GROUPS // NZ
BLOCK = R // NZ
SHARE = NDEG // NZ
STEPS = (2, 3, 1, 0)
HOME = 3


def ell_index(x, y, core):
    return (lax.rem(x + 2 * NX, NX) * NY + lax.rem(y + 2 * NY, NY)) * NC + core


def split(e):
    return lax.div(e, NY * NC), lax.rem(lax.div(e, NC), NY), lax.rem(e, NC)


def owner_of(e, z, t):
    x, y, core = split(e)
    way = 1 - 2 * core
    return ell_index(x + way * STEPS[t], y + way * (STEPS[t] + lax.div(z, NC)), lax.rem(core + z, NC))


def group_of(o, z, t):
    x, y, core = split(o)
    core = lax.rem(core + z, NC)
    way = 1 - 2 * core
    return ell_index(x - way * STEPS[t], y - way * (STEPS[t] + lax.div(z, NC)), core)


def kernel(
    owners_hbm, counts_hbm, shells_hbm, start_hbm, scale_hbm, shift_hbm, damp_hbm, out_ref,
    owners_ref, counts_ref, shells_ref, start_ref, scale_ref, shift_ref, damp_ref, load_sem,
    order, coef, coef_v, stage_start, stage_shells, got_start, got_shells, tables, rounded, sums, hopped,
    coef_sem, send_start, recv_start, send_shells, recv_shells, send_hop, recv_hop, send_out, recv_out,
):
    e, z = lax.axis_index("ell"), lax.axis_index("rad")

    def device(to_e, to_z):
        return {"ell": to_e, "rad": to_z}

    parts = 4
    loads = [
        pltpu.make_async_copy(src, dst, load_sem.at[i])
        for i, (src, dst) in enumerate(
            (
                (owners_hbm, owners_ref),
                (start_hbm, start_ref),
                (counts_hbm, counts_ref),
                (scale_hbm, scale_ref),
                (shift_hbm, shift_ref),
                (damp_hbm, damp_ref),
            )
        )
    ]
    part = GROUPS // parts
    loads += [
        pltpu.make_async_copy(
            shells_hbm.at[pl.ds(i * part, part)], shells_ref.at[pl.ds(i * part, part)], load_sem.at[6 + i]
        )
        for i in range(parts)
    ]
    for load in loads:
        load.start()

    barrier = pltpu.get_barrier_semaphore()
    for d in range(1, NZ):
        pl.semaphore_signal(barrier, inc=1, device_id=device(e, lax.rem(z + d, NZ)), device_id_type=MESH)
    stays = z == 0
    for t in range(PER):

        def greet(t=t):
            pl.semaphore_signal(barrier, inc=1, device_id=device(group_of(e, z, t), z), device_id_type=MESH)

        if t == HOME:
            pl.when(jnp.logical_not(stays))(greet)
        else:
            greet()

    loads[0].wait()
    words = [jnp.int32(0)] * (GROUPS // 4)
    for p in range(GROUPS):
        o = owners_ref[p]
        high, low = o >> 2, o & 3
        value = jnp.where(low == 0, p, jnp.where(low == 1, p << 8, jnp.where(low == 2, p << 16, p << 24)))
        for k in range(GROUPS // 4):
            words[k] = words[k] + jnp.where(high == k, value, 0)
    for k in range(GROUPS // 4):
        for b in range(4):
            order[4 * k + b] = (words[k] >> (8 * b)) & 31

    def arrive(ref, sem):
        pltpu.make_async_copy(ref, ref, sem).wait()

    def start_copy(d):
        return pltpu.make_async_remote_copy(
            src_ref=stage_start.at[d - 1],
            dst_ref=got_start.at[pl.ds(pl.multiple_of(z * 8, 8), 8)],
            send_sem=send_start,
            recv_sem=recv_start,
            device_id=device(e, lax.rem(z + d, NZ)),
            device_id_type=MESH,
        )

    def shell_copy(t, d):
        return pltpu.make_async_remote_copy(
            src_ref=stage_shells.at[d - 1, t],
            dst_ref=got_shells.at[t, pl.ds(pl.multiple_of(z * BLOCK, BLOCK), BLOCK)],
            send_sem=send_shells,
            recv_sem=recv_shells.at[t],
            device_id=device(e, lax.rem(z + d, NZ)),
            device_id_type=MESH,
        )

    far_first = (4, 3, 5, 2, 6, 1, 7)
    loads[1].wait()
    stage_start[...] = jnp.zeros_like(stage_start)
    to = [[order[owner_of(e, lax.rem(z + d, NZ), t)] for t in range(PER)] for d in range(NZ)]
    for d in range(1, NZ):
        for t in range(PER):
            stage_start[d - 1, pl.ds(t, 1), :] = start_ref[pl.ds(to[d][t], 1), :]
    for load in loads[6:]:
        load.wait()
    for d in far_first:
        stage_shells[d - 1, 0] = shells_ref[to[d][0]]
    pl.semaphore_wait(barrier, NZ - 1 + PER - stays.astype(jnp.int32))
    def send(t):
        for d in far_first:
            shell_copy(t, d).start()

    for d in far_first:
        start_copy(d).start()
    send(0)
    for t in range(1, PER):
        for d in far_first:
            stage_shells[d - 1, t] = shells_ref[to[d][t]]
        if t <= 2:
            send(t)

    mine = to[0]
    for t in range(PER):
        got_start[pl.ds(z * 8 + t, 1), :] = start_ref[pl.ds(mine[t], 1), :]
        got_shells[t, pl.ds(pl.multiple_of(z * BLOCK, BLOCK), BLOCK), :] = shells_ref[mine[t]]

    for load in loads[2:6]:
        load.wait()
    coef_v[...] = jnp.zeros_like(coef_v)
    for t in range(PER):
        for i, ref in enumerate((scale_ref, shift_ref, damp_ref)):
            coef_v[i, pl.ds(t, 1), :] = ref[pl.ds(mine[t], 1), :]
    to_scalar = pltpu.make_async_copy(coef_v, coef, coef_sem)
    to_scalar.start()

    arrive(got_start.at[pl.ds(0, (NZ - 1) * 8)], recv_start)
    to_scalar.wait()

    index = lax.broadcasted_iota(jnp.int32, (NZ, BLOCK), 0) * BLOCK + lax.broadcasted_iota(jnp.int32, (NZ, BLOCK), 1)
    nodes = jnp.cos(jnp.pi * (2.0 * index.astype(jnp.float32) + 1.0) / (2.0 * R))

    def eight(block, carry):
        carry = list(carry)
        for u in range(8):
            n = block * 8 + u
            for t in range(PER):
                before, now = carry[t]
                tables[t, block, pl.ds(u, NZ, stride=8), :] = now
                after = coef[0, t, n] * (nodes + coef[1, t, n]) * now - coef[2, t, n] * before
                carry[t] = (now, after)
        return tuple(carry)

    first = tuple((jnp.zeros((NZ, BLOCK), jnp.float32), got_start[pl.ds(t, NZ, stride=8), :]) for t in range(PER))
    lax.fori_loop(0, NDEG // 8, eight, first)

    def hop_copy(t):
        return pltpu.make_async_remote_copy(
            src_ref=sums.at[t],
            dst_ref=hopped.at[t],
            send_sem=send_hop,
            recv_sem=recv_hop.at[t],
            device_id=device(owner_of(e, z, t), z),
            device_id_type=MESH,
        )

    def hop_here(t):
        return pltpu.make_async_copy(sums.at[t], hopped.at[t], recv_hop.at[t])

    def out_copy(t, k, here=False):
        slot = group_of(e, z, t)
        src = hopped.at[t, pl.ds(k * SHARE, SHARE)]
        if here:
            return pltpu.make_async_copy(src, out_ref.at[slot], recv_out)
        return pltpu.make_async_remote_copy(
            src_ref=src,
            dst_ref=out_ref.at[slot],
            send_sem=send_out,
            recv_sem=recv_out,
            device_id=device(e, k),
            device_id_type=MESH,
        )

    def forward(t, planes):
        for k in planes:
            pl.when(z == k)(lambda k=k: out_copy(t, k, here=True).start())
            pl.when(z != k)(lambda k=k: out_copy(t, k).start())

    def hop_in(t):
        hop_here(t).wait()

    rows = 128
    for t in range(PER):
        live = counts_ref[mine[t]]

        def round_rows(step, _):
            degree = lax.broadcasted_iota(jnp.int32, (rows, BLOCK), 0) + step * rows
            for s in range(NZ):
                tall = tables[t, pl.ds(step * (rows // 8), rows // 8), pl.ds(s * 8, 8), :].reshape(rows, BLOCK)
                rounded[t, pl.ds(pl.multiple_of(step * rows, rows), rows), pl.ds(s * BLOCK, BLOCK)] = jnp.where(
                    degree < live, tall, 0.0
                ).astype(jnp.bfloat16)
            return 0

        lax.fori_loop(0, NDEG // rows, round_rows, 0)

    def work(t):
        arrive(got_shells.at[t, pl.ds(0, (NZ - 1) * BLOCK)], recv_shells.at[t])
        total = jnp.dot(rounded[t], got_shells[t], preferred_element_type=jnp.float32)
        sums[t] = total.astype(jnp.bfloat16)
        if t == HOME:
            pl.when(stays)(lambda: hop_here(HOME).start())
            pl.when(jnp.logical_not(stays))(lambda: hop_copy(HOME).start())
        else:
            hop_copy(t).start()

    work(0)
    send(3)
    work(1)
    hop_in(0)
    forward(0, (0, 1, 2, 3, 7, 6, 4, 5))
    work(2)
    hop_in(1)
    forward(1, (0, 1, 2, 3, 7, 6, 4, 5))
    work(3)
    hop_in(2)
    forward(2, (0, 1, 2, 3, 7, 6, 4, 5))
    hop_in(3)
    forward(3, (0, 1, 2, 3, 7, 6, 4, 5))
    arrive(stage_start, send_start)
    arrive(stage_shells, send_shells)
    pl.when(stays)(lambda: arrive(sums.at[pl.ds(0, PER - 1)], send_hop))
    pl.when(jnp.logical_not(stays))(lambda: arrive(sums, send_hop))
    arrive(hopped.at[:, pl.ds(0, (NZ - 1) * SHARE)], send_out)
    arrive(out_ref, recv_out)


def body(shells, start_values, rec_scale, rec_shift, rec_damp, degree_counts, owners):
    hbm = pl.BlockSpec(memory_space=pltpu.HBM)
    dma = pltpu.SemaphoreType.DMA
    arrived = pl.pallas_call(
        kernel,
        out_shape=pltpu.VMEM((GROUPS, SHARE, C), jnp.bfloat16),
        in_specs=[hbm] * 7,
        out_specs=pl.BlockSpec(memory_space=pltpu.VMEM),
        scratch_shapes=[
            pltpu.SMEM((GROUPS,), jnp.int32),
            pltpu.SMEM((GROUPS,), jnp.int32),
            pltpu.VMEM((GROUPS, BLOCK, C), jnp.bfloat16),
            pltpu.VMEM((GROUPS, BLOCK), jnp.float32),
            pltpu.VMEM((GROUPS, NDEG), jnp.float32),
            pltpu.VMEM((GROUPS, NDEG), jnp.float32),
            pltpu.VMEM((GROUPS, NDEG), jnp.float32),
            dma((10,)),
            pltpu.SMEM((GROUPS,), jnp.int32),
            pltpu.SMEM((3, 8, NDEG), jnp.float32),
            pltpu.VMEM((3, 8, NDEG), jnp.float32),
            pltpu.VMEM((NZ - 1, 8, BLOCK), jnp.float32),
            pltpu.VMEM((NZ - 1, PER, BLOCK, C), jnp.bfloat16),
            pltpu.VMEM((NZ * 8, BLOCK), jnp.float32),
            pltpu.VMEM((PER, R, C), jnp.bfloat16),
            pltpu.VMEM((PER, NDEG // 8, NZ * 8, BLOCK), jnp.float32),
            pltpu.VMEM((PER, NDEG, R), jnp.bfloat16),
            pltpu.VMEM((PER, NDEG, C), jnp.bfloat16),
            pltpu.VMEM((PER, NDEG, C), jnp.bfloat16),
            dma,
            dma,
            dma,
            dma,
            dma((PER,)),
            dma,
            dma((PER,)),
            dma,
            dma,
        ],
        compiler_params=pltpu.CompilerParams(
            collective_id=0, has_side_effects=True, vmem_limit_bytes=40 * 2**20
        ),
        name="transform",
    )(
        *(
            pltpu.with_memory_space_constraint(a, pltpu.HBM)
            for a in (owners, degree_counts, shells, start_values, rec_scale, rec_shift, rec_damp)
        )
    )
    return arrived.astype(jnp.float32)


def solution(mesh):
    return jax.shard_map(
        body,
        mesh=mesh,
        in_specs=(
            P("ell", "rad", None),
            P("ell", "rad"),
            P("ell", None),
            P("ell", None),
            P("ell", None),
            P("ell"),
            P("ell"),
        ),
        out_specs=P("ell", "rad", None),
        check_vma=False,
    )
```

```python
import jax
import jax.numpy as jnp
from jax import lax
from jax.experimental import pallas as pl
from jax.experimental.pallas import tpu as pltpu
from jax.sharding import PartitionSpec as P

MESH = pl.DeviceIdType.MESH
R = 1024
NDEG = 512
C = 128
NX, NY, NC, NZ = 4, 4, 2, 8
GROUPS = NX * NY * NC
PER = GROUPS // NZ
BLOCK = R // NZ
SHARE = NDEG // NZ
STEPS = (2, 3, 1, 0)
HOME = 3
PIECES = 8


def ell_index(x, y, core):
    return (lax.rem(x + 2 * NX, NX) * NY + lax.rem(y + 2 * NY, NY)) * NC + core


def split(e):
    return lax.div(e, NY * NC), lax.rem(lax.div(e, NC), NY), lax.rem(e, NC)


def owner_of(e, z, t):
    x, y, core = split(e)
    way = 1 - 2 * core
    return ell_index(x + way * STEPS[t], y + way * (STEPS[t] + lax.div(z, NC)), lax.rem(core + z, NC))


def group_of(o, z, t):
    x, y, core = split(o)
    core = lax.rem(core + z, NC)
    way = 1 - 2 * core
    return ell_index(x - way * STEPS[t], y - way * (STEPS[t] + lax.div(z, NC)), core)


def kernel(
    owners_hbm, counts_hbm, shells_hbm, start_hbm, scale_hbm, shift_hbm, damp_hbm, out_ref,
    owners_ref, counts_ref, shells_ref, start_ref, scale_ref, shift_ref, damp_ref, load_sem,
    order, coef, coef_v, stage_start, stage_shells, got_start, got_shells, tables, rounded, sums, hopped,
    coef_sem, send_start, recv_start, send_shells, recv_shells, send_hop, recv_hop, send_out, recv_out,
):
    e, z = lax.axis_index("ell"), lax.axis_index("rad")

    def device(to_e, to_z):
        return {"ell": to_e, "rad": to_z}

    barrier = pltpu.get_barrier_semaphore()
    for d in range(1, NZ):
        pl.semaphore_signal(barrier, inc=1, device_id=device(e, lax.rem(z + d, NZ)), device_id_type=MESH)
    stays = z == 0
    for t in range(PER):

        def greet(t=t):
            pl.semaphore_signal(barrier, inc=1, device_id=device(group_of(e, z, t), z), device_id_type=MESH)

        if t == HOME:
            pl.when(jnp.logical_not(stays))(greet)
        else:
            greet()

    parts = 4
    loads = [
        pltpu.make_async_copy(src, dst, load_sem.at[i])
        for i, (src, dst) in enumerate(
            (
                (owners_hbm, owners_ref),
                (start_hbm, start_ref),
                (counts_hbm, counts_ref),
                (scale_hbm, scale_ref),
                (shift_hbm, shift_ref),
                (damp_hbm, damp_ref),
            )
        )
    ]
    part = GROUPS // parts
    loads += [
        pltpu.make_async_copy(
            shells_hbm.at[pl.ds(i * part, part)], shells_ref.at[pl.ds(i * part, part)], load_sem.at[6 + i]
        )
        for i in range(parts)
    ]
    for load in loads:
        load.start()

    loads[0].wait()
    words = [jnp.int32(0)] * (GROUPS // 4)
    for p in range(GROUPS):
        o = owners_ref[p]
        high, low = o >> 2, o & 3
        value = jnp.where(low == 0, p, jnp.where(low == 1, p << 8, jnp.where(low == 2, p << 16, p << 24)))
        for k in range(GROUPS // 4):
            words[k] = words[k] + jnp.where(high == k, value, 0)
    for k in range(GROUPS // 4):
        for b in range(4):
            order[4 * k + b] = (words[k] >> (8 * b)) & 31

    def arrive(ref, sem):
        pltpu.make_async_copy(ref, ref, sem).wait()

    def start_copy(d):
        return pltpu.make_async_remote_copy(
            src_ref=stage_start.at[d - 1],
            dst_ref=got_start.at[pl.ds(pl.multiple_of(z * 8, 8), 8)],
            send_sem=send_start,
            recv_sem=recv_start,
            device_id=device(e, lax.rem(z + d, NZ)),
            device_id_type=MESH,
        )

    def shell_copy(t, d):
        return pltpu.make_async_remote_copy(
            src_ref=stage_shells.at[d - 1, t],
            dst_ref=got_shells.at[t, pl.ds(pl.multiple_of(z * BLOCK, BLOCK), BLOCK)],
            send_sem=send_shells,
            recv_sem=recv_shells.at[t],
            device_id=device(e, lax.rem(z + d, NZ)),
            device_id_type=MESH,
        )

    far_first = (4, 3, 5, 2, 6, 1, 7)
    loads[1].wait()
    stage_start[...] = jnp.zeros_like(stage_start)
    to = [[order[owner_of(e, lax.rem(z + d, NZ), t)] for t in range(PER)] for d in range(NZ)]
    for d in range(1, NZ):
        for t in range(PER):
            stage_start[d - 1, pl.ds(t, 1), :] = start_ref[pl.ds(to[d][t], 1), :]
    for load in loads[6:]:
        load.wait()
    for d in far_first:
        stage_shells[d - 1, 0] = shells_ref[to[d][0]]
    pl.semaphore_wait(barrier, NZ - 1 + PER - stays.astype(jnp.int32))
    def send(t):
        for d in far_first:
            shell_copy(t, d).start()

    for d in far_first:
        start_copy(d).start()
    send(0)
    for t in range(1, PER):
        for d in far_first:
            stage_shells[d - 1, t] = shells_ref[to[d][t]]
        if t <= 2:
            send(t)

    mine = to[0]
    for t in range(PER):
        got_start[pl.ds(z * 8 + t, 1), :] = start_ref[pl.ds(mine[t], 1), :]
        got_shells[t, pl.ds(pl.multiple_of(z * BLOCK, BLOCK), BLOCK), :] = shells_ref[mine[t]]

    for load in loads[2:6]:
        load.wait()
    coef_v[...] = jnp.zeros_like(coef_v)
    for t in range(PER):
        for i, ref in enumerate((scale_ref, shift_ref, damp_ref)):
            coef_v[i, pl.ds(t, 1), :] = ref[pl.ds(mine[t], 1), :]
    to_scalar = pltpu.make_async_copy(coef_v, coef, coef_sem)
    to_scalar.start()

    arrive(got_start.at[pl.ds(0, (NZ - 1) * 8)], recv_start)
    to_scalar.wait()

    index = lax.broadcasted_iota(jnp.int32, (NZ, BLOCK), 0) * BLOCK + lax.broadcasted_iota(jnp.int32, (NZ, BLOCK), 1)
    nodes = jnp.cos(jnp.pi * (2.0 * index.astype(jnp.float32) + 1.0) / (2.0 * R))

    def eight(block, carry):
        carry = list(carry)
        for u in range(8):
            n = block * 8 + u
            for t in range(PER):
                before, now = carry[t]
                tables[t, block, pl.ds(u, NZ, stride=8), :] = now
                after = coef[0, t, n] * (nodes + coef[1, t, n]) * now - coef[2, t, n] * before
                carry[t] = (now, after)
        return tuple(carry)

    first = tuple((jnp.zeros((NZ, BLOCK), jnp.float32), got_start[pl.ds(t, NZ, stride=8), :]) for t in range(PER))
    lax.fori_loop(0, NDEG // 8, eight, first)

    def hop_copy(t):
        return pltpu.make_async_remote_copy(
            src_ref=sums.at[t],
            dst_ref=hopped.at[t],
            send_sem=send_hop,
            recv_sem=recv_hop.at[t],
            device_id=device(owner_of(e, z, t), z),
            device_id_type=MESH,
        )

    def hop_here(t):
        return pltpu.make_async_copy(sums.at[t], hopped.at[t], recv_hop.at[t])

    def out_copy(t, k, here=False):
        slot = group_of(e, z, t)
        src = hopped.at[t, pl.ds(k * SHARE, SHARE)]
        if here:
            return pltpu.make_async_copy(src, out_ref.at[slot], recv_out)
        return pltpu.make_async_remote_copy(
            src_ref=src,
            dst_ref=out_ref.at[slot],
            send_sem=send_out,
            recv_sem=recv_out,
            device_id=device(e, k),
            device_id_type=MESH,
        )

    def forward(t, planes):
        for k in planes:
            pl.when(z == k)(lambda k=k: out_copy(t, k, here=True).start())
            pl.when(z != k)(lambda k=k: out_copy(t, k).start())

    def hop_in(t):
        hop_here(t).wait()

    rows = 128
    for t in range(PER):
        live = counts_ref[mine[t]]

        def round_rows(step, _):
            degree = lax.broadcasted_iota(jnp.int32, (rows, BLOCK), 0) + step * rows
            for s in range(NZ):
                tall = tables[t, pl.ds(step * (rows // 8), rows // 8), pl.ds(s * 8, 8), :].reshape(rows, BLOCK)
                rounded[t, pl.ds(pl.multiple_of(step * rows, rows), rows), pl.ds(s * BLOCK, BLOCK)] = jnp.where(
                    degree < live, tall, 0.0
                ).astype(jnp.bfloat16)
            return 0

        lax.fori_loop(0, NDEG // rows, round_rows, 0)

    def work(t):
        arrive(got_shells.at[t, pl.ds(0, (NZ - 1) * BLOCK)], recv_shells.at[t])
        total = jnp.dot(rounded[t], got_shells[t], preferred_element_type=jnp.float32)
        sums[t] = total.astype(jnp.bfloat16)
        if t == HOME:
            pl.when(stays)(lambda: hop_here(HOME).start())
            pl.when(jnp.logical_not(stays))(lambda: hop_copy(HOME).start())
        else:
            hop_copy(t).start()

    work(0)
    send(3)
    work(1)
    hop_in(0)
    forward(0, (0, 1, 2, 3, 7, 6, 4, 5))
    work(2)
    hop_in(1)
    forward(1, (0, 1, 2, 3, 7, 6, 4, 5))
    work(3)
    hop_in(2)
    forward(2, (0, 1, 2, 3, 7, 6, 4, 5))
    hop_in(3)
    forward(3, (0, 1, 2, 3, 7, 6, 4, 5))
    arrive(stage_start, send_start)
    arrive(stage_shells, send_shells)
    pl.when(stays)(lambda: arrive(sums.at[pl.ds(0, PER - 1)], send_hop))
    pl.when(jnp.logical_not(stays))(lambda: arrive(sums, send_hop))
    arrive(hopped.at[:, pl.ds(0, (NZ - 1) * SHARE)], send_out)
    arrive(out_ref, recv_out)


def widen(short_ref, long_hbm, long, sems):
    pieces = sems.shape[0]
    part = GROUPS // pieces

    def piece(i):
        rows = pl.ds(i * part, part)
        return pltpu.make_async_copy(long.at[rows], long_hbm.at[rows], sems.at[i])

    for i in range(pieces):
        rows = pl.ds(i * part, part)
        long[rows] = short_ref[rows].astype(jnp.float32)
        piece(i).start()
    for i in range(pieces):
        piece(i).wait()


def body(shells, start_values, rec_scale, rec_shift, rec_damp, degree_counts, owners):
    hbm = pl.BlockSpec(memory_space=pltpu.HBM)
    dma = pltpu.SemaphoreType.DMA
    arrived = pl.pallas_call(
        kernel,
        out_shape=pltpu.VMEM((GROUPS, SHARE, C), jnp.bfloat16),
        in_specs=[hbm] * 7,
        out_specs=pl.BlockSpec(memory_space=pltpu.VMEM),
        scratch_shapes=[
            pltpu.SMEM((GROUPS,), jnp.int32),
            pltpu.SMEM((GROUPS,), jnp.int32),
            pltpu.VMEM((GROUPS, BLOCK, C), jnp.bfloat16),
            pltpu.VMEM((GROUPS, BLOCK), jnp.float32),
            pltpu.VMEM((GROUPS, NDEG), jnp.float32),
            pltpu.VMEM((GROUPS, NDEG), jnp.float32),
            pltpu.VMEM((GROUPS, NDEG), jnp.float32),
            dma((10,)),
            pltpu.SMEM((GROUPS,), jnp.int32),
            pltpu.SMEM((3, 8, NDEG), jnp.float32),
            pltpu.VMEM((3, 8, NDEG), jnp.float32),
            pltpu.VMEM((NZ - 1, 8, BLOCK), jnp.float32),
            pltpu.VMEM((NZ - 1, PER, BLOCK, C), jnp.bfloat16),
            pltpu.VMEM((NZ * 8, BLOCK), jnp.float32),
            pltpu.VMEM((PER, R, C), jnp.bfloat16),
            pltpu.VMEM((PER, NDEG // 8, NZ * 8, BLOCK), jnp.float32),
            pltpu.VMEM((PER, NDEG, R), jnp.bfloat16),
            pltpu.VMEM((PER, NDEG, C), jnp.bfloat16),
            pltpu.VMEM((PER, NDEG, C), jnp.bfloat16),
            dma,
            dma,
            dma,
            dma,
            dma((PER,)),
            dma,
            dma((PER,)),
            dma,
            dma,
        ],
        compiler_params=pltpu.CompilerParams(
            collective_id=0, has_side_effects=True, vmem_limit_bytes=40 * 2**20
        ),
        name="transform",
    )(
        *(
            pltpu.with_memory_space_constraint(a, pltpu.HBM)
            for a in (owners, degree_counts, shells, start_values, rec_scale, rec_shift, rec_damp)
        )
    )
    return pl.pallas_call(
        widen,
        out_shape=jax.ShapeDtypeStruct((GROUPS, SHARE, C), jnp.float32),
        in_specs=[pl.BlockSpec(memory_space=pltpu.VMEM)],
        out_specs=hbm,
        scratch_shapes=[pltpu.VMEM((GROUPS, SHARE, C), jnp.float32), dma((PIECES,))],
        compiler_params=pltpu.CompilerParams(vmem_limit_bytes=40 * 2**20),
        name="widen",
    )(arrived)


def solution(mesh):
    return jax.shard_map(
        body,
        mesh=mesh,
        in_specs=(
            P("ell", "rad", None),
            P("ell", "rad"),
            P("ell", None),
            P("ell", None),
            P("ell", None),
            P("ell"),
            P("ell"),
        ),
        out_specs=P("ell", "rad", None),
        check_vma=False,
    )
```

```python
import jax
import jax.numpy as jnp
from jax import lax
from jax.experimental import pallas as pl
from jax.experimental.pallas import tpu as pltpu
from jax.sharding import PartitionSpec as P

MESH = pl.DeviceIdType.MESH
R = 1024
NDEG = 512
C = 128
NX, NY, NC, NZ = 4, 4, 2, 8
GROUPS = NX * NY * NC
PER = GROUPS // NZ
BLOCK = R // NZ
SHARE = NDEG // NZ
STEPS = (2, 3, 1, 0)
HOME = 3


def ell_index(x, y, core):
    return (lax.rem(x + 2 * NX, NX) * NY + lax.rem(y + 2 * NY, NY)) * NC + core


def split(e):
    return lax.div(e, NY * NC), lax.rem(lax.div(e, NC), NY), lax.rem(e, NC)


def owner_of(e, z, t):
    x, y, core = split(e)
    way = 1 - 2 * core
    return ell_index(x + way * STEPS[t], y + way * (STEPS[t] + lax.div(z, NC)), lax.rem(core + z, NC))


def group_of(o, z, t):
    x, y, core = split(o)
    core = lax.rem(core + z, NC)
    way = 1 - 2 * core
    return ell_index(x - way * STEPS[t], y - way * (STEPS[t] + lax.div(z, NC)), core)


def kernel(
    owners_hbm, counts_hbm, shells_hbm, start_hbm, scale_hbm, shift_hbm, damp_hbm, out_ref,
    owners_ref, counts_ref, shells_ref, start_ref, scale_ref, shift_ref, damp_ref, load_sem,
    order, coef, coef_v, stage_start, stage_shells, got_start, got_shells, tables, rounded, sums, hopped,
    coef_sem, send_start, recv_start, send_shells, recv_shells, send_hop, recv_hop, send_out, recv_out,
):
    e, z = lax.axis_index("ell"), lax.axis_index("rad")

    def device(to_e, to_z):
        return {"ell": to_e, "rad": to_z}

    barrier = pltpu.get_barrier_semaphore()
    for d in range(1, NZ):
        pl.semaphore_signal(barrier, inc=1, device_id=device(e, lax.rem(z + d, NZ)), device_id_type=MESH)
    stays = z == 0
    for t in range(PER):

        def greet(t=t):
            pl.semaphore_signal(barrier, inc=1, device_id=device(group_of(e, z, t), z), device_id_type=MESH)

        if t == HOME:
            pl.when(jnp.logical_not(stays))(greet)
        else:
            greet()

    parts = 4
    loads = [
        pltpu.make_async_copy(src, dst, load_sem.at[i])
        for i, (src, dst) in enumerate(
            (
                (owners_hbm, owners_ref),
                (start_hbm, start_ref),
                (counts_hbm, counts_ref),
                (scale_hbm, scale_ref),
                (shift_hbm, shift_ref),
                (damp_hbm, damp_ref),
            )
        )
    ]
    part = GROUPS // parts
    loads += [
        pltpu.make_async_copy(
            shells_hbm.at[pl.ds(i * part, part)], shells_ref.at[pl.ds(i * part, part)], load_sem.at[6 + i]
        )
        for i in range(parts)
    ]
    for load in loads:
        load.start()

    loads[0].wait()
    words = [jnp.int32(0)] * (GROUPS // 4)
    for p in range(GROUPS):
        o = owners_ref[p]
        high, low = o >> 2, o & 3
        value = jnp.where(low == 0, p, jnp.where(low == 1, p << 8, jnp.where(low == 2, p << 16, p << 24)))
        for k in range(GROUPS // 4):
            words[k] = words[k] + jnp.where(high == k, value, 0)
    for k in range(GROUPS // 4):
        for b in range(4):
            order[4 * k + b] = (words[k] >> (8 * b)) & 31

    def arrive(ref, sem):
        pltpu.make_async_copy(ref, ref, sem).wait()

    def start_copy(d):
        return pltpu.make_async_remote_copy(
            src_ref=stage_start.at[d - 1],
            dst_ref=got_start.at[pl.ds(pl.multiple_of(z * 8, 8), 8)],
            send_sem=send_start,
            recv_sem=recv_start,
            device_id=device(e, lax.rem(z + d, NZ)),
            device_id_type=MESH,
        )

    def shell_copy(t, d):
        return pltpu.make_async_remote_copy(
            src_ref=stage_shells.at[d - 1, t],
            dst_ref=got_shells.at[t, pl.ds(pl.multiple_of(z * BLOCK, BLOCK), BLOCK)],
            send_sem=send_shells,
            recv_sem=recv_shells.at[t],
            device_id=device(e, lax.rem(z + d, NZ)),
            device_id_type=MESH,
        )

    far_first = (4, 5, 3, 6, 2, 7, 1)
    loads[1].wait()
    stage_start[...] = jnp.zeros_like(stage_start)
    to = [[order[owner_of(e, lax.rem(z + d, NZ), t)] for t in range(PER)] for d in range(NZ)]
    for d in range(1, NZ):
        for t in range(PER):
            stage_start[d - 1, pl.ds(t, 1), :] = start_ref[pl.ds(to[d][t], 1), :]
    for load in loads[6:]:
        load.wait()
    for d in far_first:
        stage_shells[d - 1, 0] = shells_ref[to[d][0]]
    pl.semaphore_wait(barrier, NZ - 1 + PER - stays.astype(jnp.int32))
    def send(t):
        for d in far_first:
            shell_copy(t, d).start()

    for d in far_first:
        start_copy(d).start()
    send(0)
    for t in range(1, PER):
        for d in far_first:
            stage_shells[d - 1, t] = shells_ref[to[d][t]]
        if t <= 2:
            send(t)

    mine = to[0]
    for t in range(PER):
        got_start[pl.ds(z * 8 + t, 1), :] = start_ref[pl.ds(mine[t], 1), :]
        got_shells[t, pl.ds(pl.multiple_of(z * BLOCK, BLOCK), BLOCK), :] = shells_ref[mine[t]]

    for load in loads[2:6]:
        load.wait()
    coef_v[...] = jnp.zeros_like(coef_v)
    for t in range(PER):
        for i, ref in enumerate((scale_ref, shift_ref, damp_ref)):
            coef_v[i, pl.ds(t, 1), :] = ref[pl.ds(mine[t], 1), :]
    to_scalar = pltpu.make_async_copy(coef_v, coef, coef_sem)
    to_scalar.start()

    arrive(got_start.at[pl.ds(0, (NZ - 1) * 8)], recv_start)
    to_scalar.wait()

    index = lax.broadcasted_iota(jnp.int32, (NZ, BLOCK), 0) * BLOCK + lax.broadcasted_iota(jnp.int32, (NZ, BLOCK), 1)
    nodes = jnp.cos(jnp.pi * (2.0 * index.astype(jnp.float32) + 1.0) / (2.0 * R))

    def eight(block, carry):
        carry = list(carry)
        for u in range(8):
            n = block * 8 + u
            for t in range(PER):
                before, now = carry[t]
                tables[t, block, pl.ds(u, NZ, stride=8), :] = now
                after = coef[0, t, n] * (nodes + coef[1, t, n]) * now - coef[2, t, n] * before
                carry[t] = (now, after)
        return tuple(carry)

    first = tuple((jnp.zeros((NZ, BLOCK), jnp.float32), got_start[pl.ds(t, NZ, stride=8), :]) for t in range(PER))
    lax.fori_loop(0, NDEG // 8, eight, first)

    def hop_copy(t):
        return pltpu.make_async_remote_copy(
            src_ref=sums.at[t],
            dst_ref=hopped.at[t],
            send_sem=send_hop,
            recv_sem=recv_hop.at[t],
            device_id=device(owner_of(e, z, t), z),
            device_id_type=MESH,
        )

    def hop_here(t):
        return pltpu.make_async_copy(sums.at[t], hopped.at[t], recv_hop.at[t])

    def out_copy(t, k, here=False):
        slot = group_of(e, z, t)
        src = hopped.at[t, pl.ds(k * SHARE, SHARE)]
        if here:
            return pltpu.make_async_copy(src, out_ref.at[slot], recv_out)
        return pltpu.make_async_remote_copy(
            src_ref=src,
            dst_ref=out_ref.at[slot],
            send_sem=send_out,
            recv_sem=recv_out,
            device_id=device(e, k),
            device_id_type=MESH,
        )

    def forward(t, planes):
        for k in planes:
            pl.when(z == k)(lambda k=k: out_copy(t, k, here=True).start())
            pl.when(z != k)(lambda k=k: out_copy(t, k).start())

    def hop_in(t):
        hop_here(t).wait()

    rows = 128
    for t in range(PER):
        live = counts_ref[mine[t]]

        def round_rows(step, _):
            degree = lax.broadcasted_iota(jnp.int32, (rows, BLOCK), 0) + step * rows
            for s in range(NZ):
                tall = tables[t, pl.ds(step * (rows // 8), rows // 8), pl.ds(s * 8, 8), :].reshape(rows, BLOCK)
                rounded[t, pl.ds(pl.multiple_of(step * rows, rows), rows), pl.ds(s * BLOCK, BLOCK)] = jnp.where(
                    degree < live, tall, 0.0
                ).astype(jnp.bfloat16)
            return 0

        lax.fori_loop(0, NDEG // rows, round_rows, 0)

    def work(t):
        arrive(got_shells.at[t, pl.ds(0, (NZ - 1) * BLOCK)], recv_shells.at[t])
        total = jnp.dot(rounded[t], got_shells[t], preferred_element_type=jnp.float32)
        sums[t] = total.astype(jnp.bfloat16)
        if t == HOME:
            pl.when(stays)(lambda: hop_here(HOME).start())
            pl.when(jnp.logical_not(stays))(lambda: hop_copy(HOME).start())
        else:
            hop_copy(t).start()

    work(0)
    send(3)
    work(1)
    hop_in(0)
    forward(0, (0, 1, 2, 3, 7, 6, 4, 5))
    work(2)
    hop_in(1)
    forward(1, (0, 1, 2, 3, 7, 6, 4, 5))
    work(3)
    hop_in(2)
    forward(2, (0, 1, 2, 3, 7, 6, 4, 5))
    hop_in(3)
    forward(3, (0, 1, 2, 3, 7, 6, 4, 5))
    arrive(stage_start, send_start)
    arrive(stage_shells, send_shells)
    pl.when(stays)(lambda: arrive(sums.at[pl.ds(0, PER - 1)], send_hop))
    pl.when(jnp.logical_not(stays))(lambda: arrive(sums, send_hop))
    arrive(hopped.at[:, pl.ds(0, (NZ - 1) * SHARE)], send_out)
    arrive(out_ref, recv_out)


def body(shells, start_values, rec_scale, rec_shift, rec_damp, degree_counts, owners):
    hbm = pl.BlockSpec(memory_space=pltpu.HBM)
    dma = pltpu.SemaphoreType.DMA
    arrived = pl.pallas_call(
        kernel,
        out_shape=pltpu.VMEM((GROUPS, SHARE, C), jnp.bfloat16),
        in_specs=[hbm] * 7,
        out_specs=pl.BlockSpec(memory_space=pltpu.VMEM),
        scratch_shapes=[
            pltpu.SMEM((GROUPS,), jnp.int32),
            pltpu.SMEM((GROUPS,), jnp.int32),
            pltpu.VMEM((GROUPS, BLOCK, C), jnp.bfloat16),
            pltpu.VMEM((GROUPS, BLOCK), jnp.float32),
            pltpu.VMEM((GROUPS, NDEG), jnp.float32),
            pltpu.VMEM((GROUPS, NDEG), jnp.float32),
            pltpu.VMEM((GROUPS, NDEG), jnp.float32),
            dma((10,)),
            pltpu.SMEM((GROUPS,), jnp.int32),
            pltpu.SMEM((3, 8, NDEG), jnp.float32),
            pltpu.VMEM((3, 8, NDEG), jnp.float32),
            pltpu.VMEM((NZ - 1, 8, BLOCK), jnp.float32),
            pltpu.VMEM((NZ - 1, PER, BLOCK, C), jnp.bfloat16),
            pltpu.VMEM((NZ * 8, BLOCK), jnp.float32),
            pltpu.VMEM((PER, R, C), jnp.bfloat16),
            pltpu.VMEM((PER, NDEG // 8, NZ * 8, BLOCK), jnp.float32),
            pltpu.VMEM((PER, NDEG, R), jnp.bfloat16),
            pltpu.VMEM((PER, NDEG, C), jnp.bfloat16),
            pltpu.VMEM((PER, NDEG, C), jnp.bfloat16),
            dma,
            dma,
            dma,
            dma,
            dma((PER,)),
            dma,
            dma((PER,)),
            dma,
            dma,
        ],
        compiler_params=pltpu.CompilerParams(
            collective_id=0, has_side_effects=True, vmem_limit_bytes=40 * 2**20
        ),
        name="transform",
    )(
        *(
            pltpu.with_memory_space_constraint(a, pltpu.HBM)
            for a in (owners, degree_counts, shells, start_values, rec_scale, rec_shift, rec_damp)
        )
    )
    return arrived.astype(jnp.float32)


def solution(mesh):
    return jax.shard_map(
        body,
        mesh=mesh,
        in_specs=(
            P("ell", "rad", None),
            P("ell", "rad"),
            P("ell", None),
            P("ell", None),
            P("ell", None),
            P("ell"),
            P("ell"),
        ),
        out_specs=P("ell", "rad", None),
        check_vma=False,
    )
```
